768 devices in a mesh: ctx: 96 (over y_hi, z, core), tp: 8 (over x, y_lo).
Axes of the slice: x: 4, y: 8 (y_hi: 4, y_lo: 2; y = y_hi * 2 + y_lo), z: 12, core: 2. Of those that a mesh axis runs over, the one named last changes fastest.
Arguments:
- queries: bfloat16 [49152, 4096], P('ctx', 'tp'), may hold values from -140 to 140
- key_vecs: bfloat16 [49152, 1024], P('ctx', 'tp'), may hold values from -6 to 6
- value_vecs: bfloat16 [49152, 1024], P('ctx', 'tp'), may hold values from -6 to 6
- out_grad: bfloat16 [49152, 4096], P('ctx', 'tp'), may hold values from -6 to 6
- doc_ids: int32 [384], replicated, may hold values from 0 to 127, never falling along the last dimension, each value on 1 to 8 neighbouring positions
Outputs:
- attended: bfloat16 [49152, 4096], P('ctx', 'tp')
- query_grad: bfloat16 [49152, 4096], P('ctx', 'tp')
- key_grad: bfloat16 [49152, 1024], P('ctx', 'tp')
- value_grad: bfloat16 [49152, 1024], P('ctx', 'tp')
The draws below stay inside these ranges and needn't reach their ends.
Inputs may be any that keep to these rules, and one draw needn't show every extreme that they name: doc_ids never fall along the sequence; each document covers 1 to 8 blocks and one covers exactly 8.
All inputs are finite; a program needn't handle non-finite values.
Results may differ from the reference program's by a relative error of at most 0.0075.
Values may be sent and summed in bfloat16 or wider, within the bound.
A program may use at most 64 MiB of HBM per device.

```python
import math
import jax
import jax.numpy as jnp
import numpy as np
from jax import lax

QH = 32
KVH = 8
HD = 128
BLK = 128
REACH = 2
TOK_DEV = 512
TOKENS = 49152
NBLK = 384
MOST_BLK = 8
DOCS = 128
N_CTX = 96


def joint_draw(key):
    noise_query = jnp.clip(jax.random.normal(jax.random.fold_in(key, 11), (TOKENS, QH * HD), jnp.float32), -6.0, 6.0)
    noise_key = jnp.clip(jax.random.normal(jax.random.fold_in(key, 12), (TOKENS, KVH * HD), jnp.float32), -6.0, 6.0)
    return (noise_query, noise_key)


def draw_queries(key, part):
    return joint_draw(key)[0].astype(jnp.bfloat16)


def draw_key_vecs(key, part):
    return joint_draw(key)[1].astype(jnp.bfloat16)


def draw_out_grad(key, part):
    noise_grad = jnp.clip(jax.random.normal(jax.random.fold_in(key, 21), (TOKENS, QH * HD), jnp.float32), -6.0, 6.0)
    return noise_grad.astype(jnp.bfloat16)


def levels(stream_key, dims, split, low, high):
    def one(axis_at, shards_of):
        heights = jax.random.uniform(jax.random.fold_in(jax.random.fold_in(stream_key, 6), axis_at), (shards_of,), jnp.float32, low / len(split), high / len(split))
        return jnp.repeat(jnp.exp(heights), dims[axis_at] // shards_of).reshape((-1,) + (1,) * (len(dims) - axis_at - 1))

    gain = one(*split[0])
    for cut in split[1:]:
        gain = gain * one(*cut)
    return gain


def split_up(number_of, total, limit, lean):
    portions = [(1 << 20) // math.isqrt(rank ** lean) + 1 for rank in range(2, number_of + 1)]
    rest, holding = total - limit - (number_of - 1), [1] * (number_of - 1)
    while rest > 0:
        candidates = [i for i in range(number_of - 1) if holding[i] < limit]
        mass, budget = sum([portions[i] for i in candidates]), rest
        for i in candidates:
            more = min(limit - holding[i], max(1, budget * portions[i] // mass), rest)
            holding[i] = holding[i] + more
            rest = rest - more
    return np.array([limit] + holding)


def ragged(key, number_of, total, reach, slope):
    if number_of == 2:
        one = jax.random.randint(key, (), max(1, total - reach), min(reach, total - 1) + 1)
        return jnp.stack([one, total - one])
    tallies = jnp.asarray(split_up(number_of, total, reach, slope), jnp.int32)
    pairs = (number_of - 1) // 2
    giver, sink = tallies[1:1 + 2 * pairs:2], tallies[2:2 + 2 * pairs:2]
    room = jnp.minimum(giver - 1, reach - sink)
    moved = jax.random.randint(jax.random.fold_in(key, 1), (pairs,), 0, 1 << 20) % (room + 1)
    tallies = tallies.at[1:1 + 2 * pairs:2].set(giver - moved).at[2:2 + 2 * pairs:2].set(sink + moved)
    return tallies[jax.random.permutation(jax.random.fold_in(key, 2), number_of)]


def bell_draw(own_key, dims, width, limit, split=(), kind=jnp.bfloat16):
    array = jax.random.normal(own_key, dims, jnp.float32) * width
    if len(split) > 0:
        array = levels(own_key, dims, split, -0.22, 0.18) * array
    return jnp.clip(array, min=-limit, max=limit).astype(kind)


def setup_inputs(seed: int = 0) -> dict:
    streams_of = jax.random.split(jax.random.key(seed), 6)
    return {
        "queries": draw_queries(jax.random.fold_in(streams_of[5], 71), 0),
        "key_vecs": draw_key_vecs(jax.random.fold_in(streams_of[5], 71), 0),
        "value_vecs": bell_draw(streams_of[2], (TOKENS, KVH * HD), 1.0, 6.0, ((0, 96), (1, 8))),
        "out_grad": draw_out_grad(jax.random.fold_in(streams_of[5], 71), 0),
        "doc_ids": jnp.searchsorted(jnp.cumsum(ragged(streams_of[4], DOCS, NBLK, MOST_BLK, 2)), jnp.arange(NBLK), side="right").astype(jnp.int32),
    }


negative_fill = -1.0e30


def reference(queries, key_vecs, value_vecs, out_grad, doc_ids):
    length_dev = TOK_DEV
    window = (REACH + 1) * length_dev
    lead = REACH * length_dev
    group_size = QH // KVH
    scale_factor = HD ** -0.5
    blocks_dev = length_dev // BLK
    zero_rows = jnp.zeros((lead, KVH * HD), jnp.bfloat16)
    keys_pad = jnp.concatenate([zero_rows, key_vecs], axis=0)
    values_pad = jnp.concatenate([zero_rows, value_vecs], axis=0)
    docs_pad = jnp.concatenate([jnp.full((REACH * blocks_dev,), -1, jnp.int32), doc_ids.astype(jnp.int32)])

    def step(carry, index):
        key_acc, value_acc = carry
        start = (index * length_dev).astype(jnp.int32)
        query_part = lax.dynamic_slice_in_dim(queries, start, length_dev, 0).astype(jnp.float32).reshape(length_dev, KVH, group_size, HD)
        grad_part = lax.dynamic_slice_in_dim(out_grad, start, length_dev, 0).astype(jnp.float32).reshape(length_dev, KVH, group_size, HD)
        key_part = lax.dynamic_slice_in_dim(keys_pad, start, window, 0).astype(jnp.float32).reshape(window, KVH, HD)
        value_part = lax.dynamic_slice_in_dim(values_pad, start, window, 0).astype(jnp.float32).reshape(window, KVH, HD)
        block_start = (index * blocks_dev).astype(jnp.int32)
        query_docs = jnp.repeat(lax.dynamic_slice_in_dim(doc_ids.astype(jnp.int32), block_start, blocks_dev, 0), BLK)
        key_docs = jnp.repeat(lax.dynamic_slice_in_dim(docs_pad, block_start, window // BLK, 0), BLK)
        query_pos = start + jnp.arange(length_dev, dtype=jnp.int32)
        key_pos = start - lead + jnp.arange(window, dtype=jnp.int32)
        allowed = (query_docs[:, None] == key_docs[None, :]) & (key_pos[None, :] <= query_pos[:, None]) & (key_pos[None, :] >= 0)
        scores = jnp.einsum("qhgd,khd->hgqk", query_part, key_part) * scale_factor
        highest = jnp.max(jnp.where(allowed, scores, negative_fill), axis=-1, keepdims=True)
        total = jnp.sum(jnp.where(allowed, jnp.exp(scores - highest), 0.0), axis=-1, keepdims=True)
        lse = highest + jnp.log(total)
        probs = jnp.where(allowed, jnp.exp(scores - lse), 0.0)
        probs16 = probs.astype(jnp.bfloat16)
        output = jnp.einsum("hgqk,khd->qhgd", probs16.astype(jnp.float32), value_part)
        output16 = output.astype(jnp.bfloat16)
        delta = jnp.sum(grad_part * output16.astype(jnp.float32), axis=-1)
        delta_hgq = jnp.transpose(delta, (1, 2, 0))
        dprobs = jnp.einsum("qhgd,khd->hgqk", grad_part, value_part)
        dscores = (probs * (dprobs - delta_hgq[..., None])).astype(jnp.bfloat16).astype(jnp.float32)
        query_grad = jnp.einsum("hgqk,khd->qhgd", dscores, key_part) * scale_factor
        key_term = jnp.einsum("hgqk,qhgd->khd", dscores, query_part) * scale_factor
        value_term = jnp.einsum("hgqk,qhgd->khd", probs16.astype(jnp.float32), grad_part)
        key_acc = lax.dynamic_update_slice_in_dim(key_acc, lax.dynamic_slice_in_dim(key_acc, start, window, 0) + key_term.reshape(window, KVH * HD), start, 0)
        value_acc = lax.dynamic_update_slice_in_dim(value_acc, lax.dynamic_slice_in_dim(value_acc, start, window, 0) + value_term.reshape(window, KVH * HD), start, 0)
        return (key_acc, value_acc), (output16.reshape(length_dev, QH * HD), query_grad.astype(jnp.bfloat16).reshape(length_dev, QH * HD))

    start_acc = jnp.zeros((lead + TOKENS, KVH * HD), jnp.float32)
    (key_acc, value_acc), (outputs, query_grads) = lax.scan(step, (start_acc, start_acc), jnp.arange(N_CTX, dtype=jnp.int32))
    attended = outputs.reshape(TOKENS, QH * HD)
    query_grad = query_grads.reshape(TOKENS, QH * HD)
    key_grad = key_acc[lead:].astype(jnp.bfloat16)
    value_grad = value_acc[lead:].astype(jnp.bfloat16)
    return (attended, query_grad, key_grad, value_grad)
```

```python
import functools
import math

import jax
import jax.numpy as jnp
from jax import lax
from jax.experimental import pallas as pl
from jax.experimental.pallas import tpu as pltpu
from jax.sharding import PartitionSpec as P

HD = 128
BLK = 128
HEADS = 4
NB = 4
TOK = NB * BLK
WIN = 11
COLS = HEADS * BLK
OWN = 7 * BLK
ONE = 3 * BLK
SCALE = HD**-0.5
SCALE2 = SCALE * math.log2(math.e)
MESH = pl.DeviceIdType.MESH
F32 = jnp.float32
BF16 = jnp.bfloat16


def dot(a, b):
    return jnp.dot(a, b, preferred_element_type=F32)


def kernel(
    n,
    docs, q_hbm, k_hbm, v_hbm, g_hbm,
    att_out, qg_out, kg_out, vg_out,
    q_in, g_in,
    kwin, vwin, k_t, v_t, q_t, g_t, q_s, g_s,
    e_all, p_all, d_all, top, total, alpha, delta,
    dk_own, dv_own, pk, pv, rk1, rk2, rv1, rv2,
    load_sem, send_sem, recv_sem, back_send, back_recv,
):
    s = lax.axis_index("ctx")
    even = lax.rem(s, 2) == 0
    odd = lax.rem(s, 2) == 1
    prev1, prev2, next1, next2 = s >= 1, s >= 2, s + 1 < n, s + 2 < n

    def to(shift):
        return {"ctx": lax.rem(s + shift + n, n)}

    barrier = pltpu.get_barrier_semaphore()

    @pl.when(prev1)
    def _():
        pl.semaphore_signal(barrier, inc=1, device_id=to(-1), device_id_type=MESH)

    @pl.when(prev2 & even)
    def _():
        pl.semaphore_signal(barrier, inc=1, device_id=to(-2), device_id_type=MESH)

    own = pl.ds(OWN, TOK)
    load_q = pltpu.make_async_copy(q_hbm, q_in, load_sem.at[0])
    load_k = pltpu.make_async_copy(k_hbm, kwin.at[own], load_sem.at[1])
    load_v = pltpu.make_async_copy(v_hbm, vwin.at[own], load_sem.at[2])
    load_g = pltpu.make_async_copy(g_hbm, g_in, load_sem.at[3])

    targets = next1.astype(jnp.int32) + (next2 & even).astype(jnp.int32)

    @pl.when(targets > 0)
    def _():
        pl.semaphore_wait(barrier, targets)

    def send(src, dst, i, shift):
        return pltpu.make_async_remote_copy(
            src, dst, send_sem.at[i], recv_sem.at[i], device_id=to(shift), device_id_type=MESH
        )

    tail = pl.ds(BLK, 3 * BLK)
    one, two, one_tail = pl.ds(ONE, TOK), pl.ds(0, 3 * BLK), pl.ds(ONE + BLK, 3 * BLK)
    k1 = send(k_hbm, kwin.at[one], 0, 1)
    v1 = send(v_hbm, vwin.at[one], 2, 1)
    k2 = send(k_hbm.at[tail], kwin.at[two], 1, 2)
    v2 = send(v_hbm.at[tail], vwin.at[two], 3, 2)
    k2_on = send(kwin.at[one_tail], kwin.at[two], 1, 1)
    v2_on = send(vwin.at[one_tail], vwin.at[two], 3, 1)

    @pl.when(next1)
    def _():
        k1.start()

    @pl.when(next2 & even)
    def _():
        k2.start()

    @pl.when(next1)
    def _():
        v1.start()

    @pl.when(next2 & even)
    def _():
        v2.start()

    for load in (load_q, load_k, load_g, load_v):
        load.start()

    @pl.when(jnp.logical_not(prev1))
    def _():
        kwin[one] = jnp.zeros((TOK, HD), BF16)
        vwin[one] = jnp.zeros((TOK, HD), BF16)

    @pl.when(jnp.logical_not(prev2))
    def _():
        kwin[two] = jnp.zeros((3 * BLK, HD), BF16)
        vwin[two] = jnp.zeros((3 * BLK, HD), BF16)

    def cut(i):
        return slice(i * BLK, (i + 1) * BLK)

    def cols(b):
        return slice(b * COLS, (b + 1) * COLS)

    def split(src, stacked, turned):
        for b in range(NB):
            for h in range(HEADS):
                x = src[cut(b), cut(h)]
                at = slice(b * COLS + h * BLK, b * COLS + (h + 1) * BLK)
                stacked[at, :] = x
                turned[:, at] = x.T

    def turn(src, dst, rows):
        dst[:, rows] = src[rows, :].T

    causal = lax.broadcasted_iota(jnp.int32, (BLK, COLS), 0) <= lax.rem(
        lax.broadcasted_iota(jnp.int32, (BLK, COLS), 1), BLK
    )

    def score(w, b):
        x = dot(kwin[cut(w), :], q_t[:, cols(b)])
        if w == b + 7:
            x = jnp.where(causal, x, -1e30)
        m = jnp.max(x, axis=0, keepdims=True)
        e = jnp.exp2((x - m) * SCALE2)
        top[w : w + 1, cols(b)] = m
        total[w : w + 1, cols(b)] = jnp.sum(e, axis=0, keepdims=True)
        e_all[cut(w), cols(b)] = e

    def reach(w):
        return [b for b in range(NB) if b <= w <= b + 7]

    load_q.wait()
    split(q_in, q_s, q_t)
    load_k.wait()
    for w in range(7, 11):
        for b in reach(w):
            score(w, b)
    turn(kwin, k_t, slice(OWN, OWN + TOK))
    load_g.wait()
    split(g_in, g_s, g_t)
    load_v.wait()
    turn(vwin, v_t, slice(OWN, OWN + TOK))

    @pl.when(prev1)
    def _():
        k1.wait_recv()

    @pl.when(prev1 & next1 & even)
    def _():
        k2_on.start()

    for b in range(NB):
        for w in range(3, 7):
            score(w, b)
    turn(kwin, k_t, slice(ONE, ONE + TOK))

    @pl.when(prev2)
    def _():
        k2.wait_recv()

    for w in range(3):
        for b in reach(w):
            score(w, b)
    turn(kwin, k_t, slice(0, 3 * BLK))

    for b in range(NB):
        mine = docs[s * NB + b]
        ws = range(b, b + 8)
        alike = []
        for w in ws:
            at = s * NB + (w - 7)
            alike.append((docs[jnp.maximum(at, 0)] == mine) & (at >= 0))
        tops = [top[w : w + 1, cols(b)] for w in ws]
        high = tops[-1]
        for t, ok in zip(tops[:-1], alike[:-1]):
            high = jnp.maximum(high, jnp.where(ok, t, -1e30))
        alphas = [
            jnp.where(ok, jnp.exp2((t - high) * SCALE2), 0.0) for t, ok in zip(tops, alike)
        ]
        whole = sum(a * total[w : w + 1, cols(b)] for a, w in zip(alphas, ws))
        inverse = 1.0 / whole
        for a, w in zip(alphas, ws):
            alpha[w : w + 1, cols(b)] = a * inverse

    def prob(w, b):
        p_all[cut(w), cols(b)] = (e_all[cut(w), cols(b)] * alpha[w : w + 1, cols(b)]).astype(BF16)

    def gather(pairs, other, w):
        bs = reach(w)
        at = slice(bs[0] * COLS, (bs[-1] + 1) * COLS)
        return dot(pairs[cut(w), at], other[at, :])

    def back(src, dst, i, shift):
        return pltpu.make_async_remote_copy(
            src, dst, back_send.at[i], back_recv.at[i], device_id=to(shift), device_id_type=MESH
        )

    pv1 = back(pv.at[one], rv1, 0, -1)
    pv2 = back(pv.at[two], rv2, 1, -2)
    pk1 = back(pk.at[one], rk1, 2, -1)
    pk2 = back(pk.at[two], rk2, 3, -2)

    for w in range(7):
        for b in reach(w):
            prob(w, b)
    for w in range(3, 7):
        pv[cut(w), :] = gather(p_all, g_s, w).astype(BF16)

    @pl.when(prev1)
    def _():
        pv1.start()

    for w in range(3):
        pv[cut(w), :] = gather(p_all, g_s, w).astype(BF16)

    @pl.when(prev2)
    def _():
        pv2.start()

    for w in range(7, 11):
        for b in reach(w):
            prob(w, b)

    @pl.when(prev1)
    def _():
        v1.wait_recv()

    @pl.when(prev1 & next1 & even)
    def _():
        v2_on.start()

    turn(vwin, v_t, slice(ONE, ONE + TOK))

    @pl.when(prev2)
    def _():
        v2.wait_recv()

    turn(vwin, v_t, slice(0, 3 * BLK))

    def home(dst, b, x):
        for h in range(HEADS):
            dst[cut(b), cut(h)] = x[:, cut(h)].T

    for b in range(NB):
        keys = slice(b * BLK, (b + 8) * BLK)
        out = dot(v_t[:, keys], p_all[keys, cols(b)]).astype(BF16)
        delta[0:1, cols(b)] = jnp.sum(
            g_t[:, cols(b)].astype(F32) * out.astype(F32), axis=0, keepdims=True
        )
        home(att_out, b, out)

    def dscore(w, b):
        dp = dot(vwin[cut(w), :], g_t[:, cols(b)])
        d_all[cut(w), cols(b)] = (
            p_all[cut(w), cols(b)].astype(F32) * (dp - delta[0:1, cols(b)])
        ).astype(BF16)

    for w in range(7):
        for b in reach(w):
            dscore(w, b)
    for w in range(3, 7):
        pk[cut(w), :] = (gather(d_all, q_s, w) * SCALE).astype(BF16)

    @pl.when(prev1)
    def _():
        pk1.start()

    for w in range(3):
        pk[cut(w), :] = (gather(d_all, q_s, w) * SCALE).astype(BF16)

    @pl.when(prev2)
    def _():
        pk2.start()

    for w in range(7, 11):
        for b in reach(w):
            dscore(w, b)
    for b in range(NB):
        keys = slice(b * BLK, (b + 8) * BLK)
        home(qg_out, b, (dot(k_t[:, keys], d_all[keys, cols(b)]) * SCALE).astype(BF16))
    for w in range(7, 11):
        dk_own[cut(w - 7), :] = gather(d_all, q_s, w) * SCALE
        dv_own[cut(w - 7), :] = gather(p_all, g_s, w)

    @pl.when(next1)
    def _():
        pv1.wait_recv()
        dv_own[...] += rv1[...].astype(F32)

    @pl.when(next2)
    def _():
        pv2.wait_recv()
        dv_own[tail] += rv2[...].astype(F32)

    vg_out[...] = dv_own[...].astype(BF16)

    @pl.when(next1)
    def _():
        pk1.wait_recv()
        dk_own[...] += rk1[...].astype(F32)

    @pl.when(next2)
    def _():
        pk2.wait_recv()
        dk_own[tail] += rk2[...].astype(F32)

    kg_out[...] = dk_own[...].astype(BF16)

    @pl.when(next1)
    def _():
        k1.wait_send()
        v1.wait_send()

    @pl.when(next2 & even)
    def _():
        k2.wait_send()
        v2.wait_send()

    @pl.when(prev1 & next1 & even)
    def _():
        k2_on.wait_send()
        v2_on.wait_send()

    @pl.when(prev1)
    def _():
        pv1.wait_send()
        pk1.wait_send()

    @pl.when(prev2)
    def _():
        pv2.wait_send()
        pk2.wait_send()


def place(*refs):
    sems = refs[-1]
    half = (len(refs) - 1) // 2
    stores = [
        pltpu.make_async_copy(refs[i], refs[half + i], sems.at[i]) for i in range(half)
    ]
    for store in stores:
        store.start()
    for store in stores:
        store.wait()


def body(n, queries, key_vecs, value_vecs, out_grad, doc_ids):
    def buf(rows, columns, kind=BF16):
        return pltpu.VMEM((rows, columns), kind)

    wide = NB * COLS
    anywhere = pl.BlockSpec(memory_space=pl.ANY)
    in_vmem = pl.BlockSpec(memory_space=pltpu.VMEM)
    sizes = [(TOK, HEADS * HD), (TOK, HEADS * HD), (TOK, HD), (TOK, HD)]
    results = pl.pallas_call(
        functools.partial(kernel, n),
        name="attention",
        out_shape=[pltpu.VMEM(size, BF16) for size in sizes],
        in_specs=[pl.BlockSpec(memory_space=pltpu.SMEM)] + [anywhere] * 4,
        out_specs=[in_vmem] * 4,
        scratch_shapes=[
            buf(TOK, HEADS * HD), buf(TOK, HEADS * HD),
            buf(WIN * BLK, HD), buf(WIN * BLK, HD), buf(HD, WIN * BLK), buf(HD, WIN * BLK),
            buf(HD, wide), buf(HD, wide), buf(wide, HD), buf(wide, HD),
            buf(WIN * BLK, wide, F32), buf(WIN * BLK, wide), buf(WIN * BLK, wide),
            buf(16, wide, F32), buf(16, wide, F32), buf(16, wide, F32), buf(8, wide, F32),
            buf(TOK, HD, F32), buf(TOK, HD, F32),
            buf(7 * BLK, HD), buf(7 * BLK, HD),
            buf(TOK, HD), buf(3 * BLK, HD), buf(TOK, HD), buf(3 * BLK, HD),
            pltpu.SemaphoreType.DMA((4,)), pltpu.SemaphoreType.DMA((4,)),
            pltpu.SemaphoreType.DMA((4,)), pltpu.SemaphoreType.DMA((4,)),
            pltpu.SemaphoreType.DMA((4,)),
        ],
        compiler_params=pltpu.CompilerParams(
            collective_id=0, has_side_effects=True, vmem_limit_bytes=56 * 1024 * 1024
        ),
        cost_estimate=pl.CostEstimate(
            flops=2 * 6 * 32 * HEADS * BLK**3, bytes_accessed=5 * TOK * TOK, transcendentals=2**21
        ),
    )(doc_ids, queries, key_vecs, value_vecs, out_grad)
    results = [pltpu.with_memory_space_constraint(r, pltpu.VMEM) for r in results]
    return pl.pallas_call(
        place,
        name="place",
        out_shape=[jax.ShapeDtypeStruct(size, BF16) for size in sizes],
        in_specs=[in_vmem] * 4,
        out_specs=[anywhere] * 4,
        scratch_shapes=[pltpu.SemaphoreType.DMA((4,))],
    )(*results)


def solution(mesh):
    placed = P("ctx", "tp")
    return jax.shard_map(
        functools.partial(body, mesh.shape["ctx"]),
        mesh=mesh,
        in_specs=(placed,) * 4 + (P(),),
        out_specs=(placed,) * 4,
        check_vma=False,
    )
```

```python
import functools
import math

import jax
import jax.numpy as jnp
from jax import lax
from jax.experimental import pallas as pl
from jax.experimental.pallas import tpu as pltpu
from jax.sharding import PartitionSpec as P

HD = 128
BLK = 128
HEADS = 4
NB = 4
TOK = NB * BLK
WIN = 11
COLS = HEADS * BLK
COLUMN = 24
OWN = 7 * BLK
ONE = 3 * BLK
SCALE = HD**-0.5
SCALE2 = SCALE * math.log2(math.e)
MESH = pl.DeviceIdType.MESH
F32 = jnp.float32
BF16 = jnp.bfloat16


def dot(a, b):
    return jnp.dot(a, b, preferred_element_type=F32)


def kernel(
    n,
    docs, q_hbm, k_hbm, v_hbm, g_hbm,
    att_out, qg_out, kg_out, vg_out,
    q_in, g_in,
    kwin, vwin, k_t, v_t, q_t, g_t, q_s, g_s,
    e_all, p_all, d_all, dp_own, out_own, top, total, alpha, delta,
    dk_own, dv_own, pk, pv, rk1, rk2, rv1, rv2,
    load_sem, send_sem, recv_sem, back_send, back_recv,
    v_hop, pv_hop, pk_hop, v_hop_send, v_hop_recv, hop_send, hop_recv, ready,
):
    s = lax.axis_index("ctx")
    even = lax.rem(s, 2) == 0
    odd = lax.rem(s, 2) == 1
    prev1, prev2, next1, next2 = s >= 1, s >= 2, s + 1 < n, s + 2 < n
    place_in = lax.rem(s, COLUMN)
    high = lax.rem(lax.axis_index("tp"), 2) == 1
    first = high & (place_in < 2) & (s >= COLUMN)
    v_passes = high & (place_in >= 2) & (place_in < 4) & (s >= COLUMN)
    passes = high & (place_in >= COLUMN - 4) & (place_in < COLUMN - 2) & (s + 4 < n)
    v_far = high & (place_in >= COLUMN - 2) & (s + 4 < n)

    def to(shift):
        return {"ctx": lax.rem(s + shift + n, n)}

    barrier = pltpu.get_barrier_semaphore()

    @pl.when(prev1)
    def _():
        pl.semaphore_signal(barrier, inc=1, device_id=to(-1), device_id_type=MESH)

    @pl.when(prev2 & even)
    def _():
        pl.semaphore_signal(barrier, inc=1, device_id=to(-2), device_id_type=MESH)

    @pl.when(first | v_passes)
    def _():
        pl.semaphore_signal(barrier, inc=1, device_id=to(-4), device_id_type=MESH)

    own = pl.ds(OWN, TOK)
    load_q = pltpu.make_async_copy(q_hbm, q_in, load_sem.at[0])
    load_k = pltpu.make_async_copy(k_hbm, kwin.at[own], load_sem.at[1])
    load_v = pltpu.make_async_copy(v_hbm, vwin.at[own], load_sem.at[2])
    load_g = pltpu.make_async_copy(g_hbm, g_in, load_sem.at[3])

    targets = sum(
        x.astype(jnp.int32) for x in (next1, next2 & even, passes, v_far)
    )

    @pl.when(targets > 0)
    def _():
        pl.semaphore_wait(barrier, targets)

    @pl.when(passes)
    def _():
        pl.semaphore_signal(ready, inc=1, device_id=to(4), device_id_type=MESH)

    def send(src, dst, i, shift):
        return pltpu.make_async_remote_copy(
            src, dst, send_sem.at[i], recv_sem.at[i], device_id=to(shift), device_id_type=MESH
        )

    tail = pl.ds(BLK, 3 * BLK)
    one, two, one_tail = pl.ds(ONE, TOK), pl.ds(0, 3 * BLK), pl.ds(ONE + BLK, 3 * BLK)
    k1 = send(k_hbm, kwin.at[one], 0, 1)
    v1 = send(v_hbm, vwin.at[one], 2, 1)
    k2 = send(k_hbm.at[tail], kwin.at[two], 1, 2)
    v2 = send(v_hbm.at[tail], vwin.at[two], 3, 2)
    k2_on = send(kwin.at[one_tail], kwin.at[two], 1, 1)
    v2_on = send(vwin.at[one_tail], vwin.at[two], 3, 1)

    @pl.when(next1)
    def _():
        k1.start()

    @pl.when(next2 & even)
    def _():
        k2.start()

    def v_up(src, i, j):
        return pltpu.make_async_remote_copy(
            v_hbm.at[src], v_hop.at[src], send_sem.at[i], v_hop_recv.at[j],
            device_id=to(4), device_id_type=MESH,
        )

    def v_over(src, dst, i, j, shift):
        return pltpu.make_async_remote_copy(
            v_hop.at[src], vwin.at[dst], v_hop_send.at[j], recv_sem.at[i],
            device_id=to(shift), device_id_type=MESH,
        )

    blocks = [pl.ds(j * BLK, BLK) for j in range(7)]
    v1_up = [v_up(blocks[j], 2, j) for j in (1, 2, 3, 0)]
    v1_over = [v_over(blocks[j], blocks[3 + j], 2, j, -3) for j in (1, 2, 3, 0)]
    v2_up = [v_up(blocks[j], 3, j) for j in (1, 2, 3)]
    v2_over = [v_over(blocks[j], blocks[j - 1], 3, j, -2) for j in (1, 2, 3)]

    @pl.when(v_far & odd)
    def _():
        for copy in v1_up:
            copy.start()

    @pl.when(v_far & even)
    def _():
        for copy in v2_up:
            copy.start()

    @pl.when(next1 & jnp.logical_not(v_far & odd))
    def _():
        v1.start()

    @pl.when(next2 & even & jnp.logical_not(v_far))
    def _():
        v2.start()

    for load in (load_q, load_k, load_g, load_v):
        load.start()

    @pl.when(jnp.logical_not(prev1))
    def _():
        kwin[one] = jnp.zeros((TOK, HD), BF16)
        vwin[one] = jnp.zeros((TOK, HD), BF16)

    @pl.when(jnp.logical_not(prev2))
    def _():
        kwin[two] = jnp.zeros((3 * BLK, HD), BF16)
        vwin[two] = jnp.zeros((3 * BLK, HD), BF16)

    def cut(i):
        return slice(i * BLK, (i + 1) * BLK)

    def cols(b):
        return slice(b * COLS, (b + 1) * COLS)

    def split(src, stacked, turned):
        for b in range(NB):
            for h in range(HEADS):
                x = src[cut(b), cut(h)]
                at = slice(b * COLS + h * BLK, b * COLS + (h + 1) * BLK)
                stacked[at, :] = x
                turned[:, at] = x.T

    def turn(src, dst, rows):
        dst[:, rows] = src[rows, :].T

    causal = lax.broadcasted_iota(jnp.int32, (BLK, COLS), 0) <= lax.rem(
        lax.broadcasted_iota(jnp.int32, (BLK, COLS), 1), BLK
    )

    def score(w, b):
        x = dot(kwin[cut(w), :], q_t[:, cols(b)])
        if w == b + 7:
            x = jnp.where(causal, x, -1e30)
        m = jnp.max(x, axis=0, keepdims=True)
        e = jnp.exp2((x - m) * SCALE2)
        top[w : w + 1, cols(b)] = m
        total[w : w + 1, cols(b)] = jnp.sum(e, axis=0, keepdims=True)
        e_all[cut(w), cols(b)] = e

    def reach(w):
        return [b for b in range(NB) if b <= w <= b + 7]

    load_q.wait()
    split(q_in, q_s, q_t)
    load_k.wait()
    for w in range(7, 11):
        for b in reach(w):
            score(w, b)
    turn(kwin, k_t, slice(OWN, OWN + TOK))
    load_g.wait()
    split(g_in, g_s, g_t)
    load_v.wait()
    turn(vwin, v_t, slice(OWN, OWN + TOK))
    for w in range(7, 11):
        for b in reach(w):
            dp_own[cut(w - 7), cols(b)] = dot(vwin[cut(w), :], g_t[:, cols(b)])

    @pl.when(prev1)
    def _():
        k1.wait_recv()

    @pl.when(prev1 & next1 & even)
    def _():
        k2_on.start()

    for b in range(NB):
        for w in range(3, 7):
            score(w, b)
    turn(kwin, k_t, slice(ONE, ONE + TOK))

    @pl.when(prev2)
    def _():
        k2.wait_recv()

    for w in range(3):
        for b in reach(w):
            score(w, b)
    turn(kwin, k_t, slice(0, 3 * BLK))

    for b in range(NB):
        mine = docs[s * NB + b]
        ws = range(b, b + 8)
        alike = []
        for w in ws:
            at = s * NB + (w - 7)
            alike.append((docs[jnp.maximum(at, 0)] == mine) & (at >= 0))
        tops = [top[w : w + 1, cols(b)] for w in ws]
        high = tops[-1]
        for t, ok in zip(tops[:-1], alike[:-1]):
            high = jnp.maximum(high, jnp.where(ok, t, -1e30))
        alphas = [
            jnp.where(ok, jnp.exp2((t - high) * SCALE2), 0.0) for t, ok in zip(tops, alike)
        ]
        whole = sum(a * total[w : w + 1, cols(b)] for a, w in zip(alphas, ws))
        inverse = 1.0 / whole
        for a, w in zip(alphas, ws):
            alpha[w : w + 1, cols(b)] = a * inverse

    def prob(w, b):
        p_all[cut(w), cols(b)] = (e_all[cut(w), cols(b)] * alpha[w : w + 1, cols(b)]).astype(BF16)

    def gather(pairs, other, w):
        bs = reach(w)
        at = slice(bs[0] * COLS, (bs[-1] + 1) * COLS)
        return dot(pairs[cut(w), at], other[at, :])

    def back(src, dst, i, shift):
        return pltpu.make_async_remote_copy(
            src, dst, back_send.at[i], back_recv.at[i], device_id=to(shift), device_id_type=MESH
        )

    pv1 = back(pv.at[one], rv1, 0, -1)
    pv2 = back(pv.at[two], rv2, 1, -2)
    pk1 = back(pk.at[one], rk1, 2, -1)
    pk2 = back(pk.at[two], rk2, 3, -2)

    def hop(src, dst, i):
        return pltpu.make_async_remote_copy(
            src, dst, back_send.at[i], hop_recv.at[i],
            device_id=to(-4), device_id_type=MESH,
        )

    def over(src, dst, i, shift):
        return pltpu.make_async_remote_copy(
            src, dst, hop_send.at[i], back_recv.at[i], device_id=to(shift), device_id_type=MESH
        )

    pv1_hop = hop(pv.at[one], pv_hop.at[one], 0)
    pv2_hop = hop(pv.at[two], pv_hop.at[two], 1)
    pk1_hop = hop(pk.at[one], pk_hop.at[one], 2)
    pk2_hop = hop(pk.at[two], pk_hop.at[two], 3)
    pv1_over = over(pv_hop.at[one], rv1, 0, 3)
    pv2_over = over(pv_hop.at[two], rv2, 1, 2)
    pk1_over = over(pk_hop.at[one], rk1, 2, 3)
    pk2_over = over(pk_hop.at[two], rk2, 3, 2)

    for w in range(7):
        for b in reach(w):
            prob(w, b)
    pv[3 * BLK :, :] = dot(p_all[3 * BLK : 7 * BLK, :], g_s[...]).astype(BF16)

    @pl.when(first)
    def _():
        pl.semaphore_wait(ready, 1)

    @pl.when(first & even)
    def _():
        pv1_hop.start()

    @pl.when(prev1 & jnp.logical_not(first & even))
    def _():
        pv1.start()

    for w in range(3):
        pv[cut(w), :] = gather(p_all, g_s, w).astype(BF16)

    @pl.when(first)
    def _():
        pv2_hop.start()

    @pl.when(prev2 & jnp.logical_not(first))
    def _():
        pv2.start()

    @pl.when(prev1)
    def _():
        v1.wait_recv()

    @pl.when(prev1 & next1 & even)
    def _():
        v2_on.start()

    for w in range(7, 11):
        for b in reach(w):
            prob(w, b)
    for b in range(NB):
        keys = slice(OWN, OWN + (b + 1) * BLK)
        out_own[:, cols(b)] = dot(v_t[:, keys], p_all[keys, cols(b)])
    turn(vwin, v_t, slice(ONE, ONE + TOK))

    @pl.when(prev2)
    def _():
        v2.wait_recv()

    turn(vwin, v_t, slice(0, 3 * BLK))

    def home(dst, b, x):
        for h in range(HEADS):
            dst[cut(b), cut(h)] = x[:, cut(h)].T

    for b in range(NB):
        keys = slice(b * BLK, OWN)
        out = (dot(v_t[:, keys], p_all[keys, cols(b)]) + out_own[:, cols(b)]).astype(BF16)
        delta[0:1, cols(b)] = jnp.sum(
            g_t[:, cols(b)].astype(F32) * out.astype(F32), axis=0, keepdims=True
        )
        home(att_out, b, out)

    def dscore(w, b):
        if w < 7:
            dp = dot(vwin[cut(w), :], g_t[:, cols(b)])
        else:
            dp = dp_own[cut(w - 7), cols(b)]
        d_all[cut(w), cols(b)] = (
            p_all[cut(w), cols(b)].astype(F32) * (dp - delta[0:1, cols(b)])
        ).astype(BF16)

    for w in range(7):
        for b in reach(w):
            dscore(w, b)
    pk[3 * BLK :, :] = (dot(d_all[3 * BLK : 7 * BLK, :], q_s[...]) * SCALE).astype(BF16)

    @pl.when(first & even)
    def _():
        pk1_hop.start()

    @pl.when(prev1 & jnp.logical_not(first & even))
    def _():
        pk1.start()

    for w in range(3):
        pk[cut(w), :] = (gather(d_all, q_s, w) * SCALE).astype(BF16)

    @pl.when(first)
    def _():
        pk2_hop.start()

    @pl.when(prev2 & jnp.logical_not(first))
    def _():
        pk2.start()

    for w in range(7, 11):
        for b in reach(w):
            dscore(w, b)
    for b in range(NB):
        keys = slice(b * BLK, (b + 8) * BLK)
        home(qg_out, b, (dot(k_t[:, keys], d_all[keys, cols(b)]) * SCALE).astype(BF16))
    for w in range(7, 11):
        dk_own[cut(w - 7), :] = gather(d_all, q_s, w) * SCALE
        dv_own[cut(w - 7), :] = gather(p_all, g_s, w)

    @pl.when(v_passes & odd)
    def _():
        for arrives, leaves in zip(v1_up, v1_over):
            arrives.wait_recv()
            leaves.start()

    @pl.when(v_passes & even)
    def _():
        for arrives, leaves in zip(v2_up, v2_over):
            arrives.wait_recv()
            leaves.start()

    @pl.when(passes & even)
    def _():
        pv1_hop.wait_recv()
        pv1_over.start()

    @pl.when(passes)
    def _():
        pv2_hop.wait_recv()
        pv2_over.start()

    @pl.when(passes & even)
    def _():
        pk1_hop.wait_recv()
        pk1_over.start()

    @pl.when(passes)
    def _():
        pk2_hop.wait_recv()
        pk2_over.start()

    @pl.when(next1)
    def _():
        pv1.wait_recv()
        dv_own[...] += rv1[...].astype(F32)

    @pl.when(next2)
    def _():
        pv2.wait_recv()
        dv_own[tail] += rv2[...].astype(F32)

    vg_out[...] = dv_own[...].astype(BF16)

    @pl.when(next1)
    def _():
        pk1.wait_recv()
        dk_own[...] += rk1[...].astype(F32)

    @pl.when(next2)
    def _():
        pk2.wait_recv()
        dk_own[tail] += rk2[...].astype(F32)

    kg_out[...] = dk_own[...].astype(BF16)

    @pl.when(next1)
    def _():
        k1.wait_send()
        v1.wait_send()

    @pl.when(next2 & even)
    def _():
        k2.wait_send()
        v2.wait_send()

    @pl.when(prev1 & next1 & even)
    def _():
        k2_on.wait_send()
        v2_on.wait_send()

    @pl.when(prev1)
    def _():
        pv1.wait_send()
        pk1.wait_send()

    @pl.when(prev2)
    def _():
        pv2.wait_send()
        pk2.wait_send()

    @pl.when(v_passes & odd)
    def _():
        for copy in v1_over:
            copy.wait_send()

    @pl.when(v_passes & even)
    def _():
        for copy in v2_over:
            copy.wait_send()

    @pl.when(passes & even)
    def _():
        pv1_over.wait_send()
        pk1_over.wait_send()

    @pl.when(passes)
    def _():
        pv2_over.wait_send()
        pk2_over.wait_send()


def place(*refs):
    sems = refs[-1]
    half = (len(refs) - 1) // 2
    stores = [
        pltpu.make_async_copy(refs[i], refs[half + i], sems.at[i]) for i in range(half)
    ]
    for store in stores:
        store.start()
    for store in stores:
        store.wait()


def body(n, queries, key_vecs, value_vecs, out_grad, doc_ids):
    def buf(rows, columns, kind=BF16):
        return pltpu.VMEM((rows, columns), kind)

    wide = NB * COLS
    anywhere = pl.BlockSpec(memory_space=pl.ANY)
    in_vmem = pl.BlockSpec(memory_space=pltpu.VMEM)
    sizes = [(TOK, HEADS * HD), (TOK, HEADS * HD), (TOK, HD), (TOK, HD)]
    results = pl.pallas_call(
        functools.partial(kernel, n),
        name="attention",
        out_shape=[pltpu.VMEM(size, BF16) for size in sizes],
        in_specs=[pl.BlockSpec(memory_space=pltpu.SMEM)] + [anywhere] * 4,
        out_specs=[in_vmem] * 4,
        scratch_shapes=[
            buf(TOK, HEADS * HD), buf(TOK, HEADS * HD),
            buf(WIN * BLK, HD), buf(WIN * BLK, HD), buf(HD, WIN * BLK), buf(HD, WIN * BLK),
            buf(HD, wide), buf(HD, wide), buf(wide, HD), buf(wide, HD),
            buf(WIN * BLK, wide, F32), buf(WIN * BLK, wide), buf(WIN * BLK, wide),
            buf(TOK, wide, F32), buf(HD, wide, F32),
            buf(16, wide, F32), buf(16, wide, F32), buf(16, wide, F32), buf(8, wide, F32),
            buf(TOK, HD, F32), buf(TOK, HD, F32),
            buf(7 * BLK, HD), buf(7 * BLK, HD),
            buf(TOK, HD), buf(3 * BLK, HD), buf(TOK, HD), buf(3 * BLK, HD),
            pltpu.SemaphoreType.DMA((4,)), pltpu.SemaphoreType.DMA((4,)),
            pltpu.SemaphoreType.DMA((4,)), pltpu.SemaphoreType.DMA((4,)),
            pltpu.SemaphoreType.DMA((4,)),
            buf(TOK, HD), buf(7 * BLK, HD), buf(7 * BLK, HD),
            pltpu.SemaphoreType.DMA((4,)), pltpu.SemaphoreType.DMA((4,)),
            pltpu.SemaphoreType.DMA((4,)), pltpu.SemaphoreType.DMA((4,)),
            pltpu.SemaphoreType.REGULAR,
        ],
        compiler_params=pltpu.CompilerParams(
            collective_id=0, has_side_effects=True, vmem_limit_bytes=56 * 1024 * 1024
        ),
        cost_estimate=pl.CostEstimate(
            flops=2 * 6 * 32 * HEADS * BLK**3, bytes_accessed=5 * TOK * TOK, transcendentals=2**21
        ),
    )(doc_ids, queries, key_vecs, value_vecs, out_grad)
    results = [pltpu.with_memory_space_constraint(r, pltpu.VMEM) for r in results]
    return pl.pallas_call(
        place,
        name="place",
        out_shape=[jax.ShapeDtypeStruct(size, BF16) for size in sizes],
        in_specs=[in_vmem] * 4,
        out_specs=[anywhere] * 4,
        scratch_shapes=[pltpu.SemaphoreType.DMA((4,))],
    )(*results)


def solution(mesh):
    placed = P("ctx", "tp")
    return jax.shard_map(
        functools.partial(body, mesh.shape["ctx"]),
        mesh=mesh,
        in_specs=(placed,) * 4 + (P(),),
        out_specs=(placed,) * 4,
        check_vma=False,
    )
```

```python
import functools
import math

import jax
import jax.numpy as jnp
from jax import lax
from jax.experimental import pallas as pl
from jax.experimental.pallas import tpu as pltpu
from jax.sharding import PartitionSpec as P

HD = 128
BLK = 128
HEADS = 4
NB = 4
TOK = NB * BLK
WIN = 11
COLS = HEADS * BLK
COLUMN = 24
OWN = 7 * BLK
ONE = 3 * BLK
SCALE = HD**-0.5
SCALE2 = SCALE * math.log2(math.e)
MESH = pl.DeviceIdType.MESH
F32 = jnp.float32
BF16 = jnp.bfloat16


def dot(a, b):
    return jnp.dot(a, b, preferred_element_type=F32)


def kernel(
    n,
    docs, q_hbm, k_hbm, v_hbm, g_hbm,
    att_out, qg_out, kg_out, vg_out,
    q_in, g_in,
    kwin, vwin, k_t, v_t, q_t, g_t, q_s, g_s,
    e_all, p_all, d_all, dp_own, out_own, top, total, alpha, delta,
    dk_own, dv_own, pk, pv, rk1, rk2, rv1, rv2,
    load_sem, send_sem, recv_sem, back_send, back_recv,
    v_hop, pv_hop, pk_hop, v_hop_send, v_hop_recv, hop_send, hop_recv, ready,
):
    s = lax.axis_index("ctx")
    even = lax.rem(s, 2) == 0
    odd = lax.rem(s, 2) == 1
    prev1, prev2, next1, next2 = s >= 1, s >= 2, s + 1 < n, s + 2 < n
    place_in = lax.rem(s, COLUMN)
    high = lax.rem(lax.axis_index("tp"), 2) == 1
    first = high & (place_in < 2) & (s >= COLUMN)
    v_passes = high & (place_in >= 2) & (place_in < 4) & (s >= COLUMN)
    passes = high & (place_in >= COLUMN - 4) & (place_in < COLUMN - 2) & (s + 4 < n)
    v_far = high & (place_in >= COLUMN - 2) & (s + 4 < n)

    def to(shift):
        return {"ctx": lax.rem(s + shift + n, n)}

    barrier = pltpu.get_barrier_semaphore()

    @pl.when(prev1)
    def _():
        pl.semaphore_signal(barrier, inc=1, device_id=to(-1), device_id_type=MESH)

    @pl.when(prev2 & even)
    def _():
        pl.semaphore_signal(barrier, inc=1, device_id=to(-2), device_id_type=MESH)

    @pl.when(first | v_passes)
    def _():
        pl.semaphore_signal(barrier, inc=1, device_id=to(-4), device_id_type=MESH)

    own = pl.ds(OWN, TOK)
    load_q = pltpu.make_async_copy(q_hbm, q_in, load_sem.at[0])
    load_k = pltpu.make_async_copy(k_hbm, kwin.at[own], load_sem.at[1])
    load_v = pltpu.make_async_copy(v_hbm, vwin.at[own], load_sem.at[2])
    load_g = pltpu.make_async_copy(g_hbm, g_in, load_sem.at[3])

    targets = sum(
        x.astype(jnp.int32) for x in (next1, next2 & even, passes, v_far)
    )

    @pl.when(targets > 0)
    def _():
        pl.semaphore_wait(barrier, targets)

    @pl.when(passes)
    def _():
        pl.semaphore_signal(ready, inc=1, device_id=to(4), device_id_type=MESH)

    def send(src, dst, i, arrival, shift):
        return pltpu.make_async_remote_copy(
            src, dst, send_sem.at[i], recv_sem.at[arrival],
            device_id=to(shift), device_id_type=MESH,
        )

    blocks = [pl.ds(j * BLK, BLK) for j in range(7)]
    tail = pl.ds(BLK, 3 * BLK)
    one, two = pl.ds(ONE, TOK), pl.ds(0, 3 * BLK)
    order = (1, 2, 3, 0)

    def stream(hbm, win, i):
        to_one = {j: send(hbm.at[blocks[j]], win.at[blocks[3 + j]], i, 7 * i + j, 1) for j in order}
        to_two = {
            j: send(hbm.at[blocks[j]], win.at[blocks[j - 1]], 2 + i, 7 * i + 3 + j, 2)
            for j in order[:3]
        }
        onward = {
            j: send(win.at[blocks[3 + j]], win.at[blocks[j - 1]], 4 + i, 7 * i + 3 + j, 1)
            for j in order[:3]
        }
        return to_one, to_two, onward

    k1, k2, k2_on = stream(k_hbm, kwin, 0)
    v1, v2, v2_on = stream(v_hbm, vwin, 1)

    def start(copies):
        for copy in copies.values():
            copy.start()

    def left(copies):
        for copy in copies.values():
            copy.wait_send()

    def arrived_one(copies, onward, j):
        @pl.when(prev1)
        def _():
            copies[j].wait_recv()

        if j > 0:

            @pl.when(prev1 & next1 & even)
            def _():
                onward[j].start()

    def arrived_two(copies, j):
        @pl.when(prev2)
        def _():
            copies[j].wait_recv()

    @pl.when(next1)
    def _():
        start(k1)

    @pl.when(next2 & even)
    def _():
        start(k2)

    def v_up(src, i, j):
        return pltpu.make_async_remote_copy(
            v_hbm.at[src], v_hop.at[src], send_sem.at[i], v_hop_recv.at[j],
            device_id=to(4), device_id_type=MESH,
        )

    def v_over(src, dst, i, j, shift):
        return pltpu.make_async_remote_copy(
            v_hop.at[src], vwin.at[dst], v_hop_send.at[j], recv_sem.at[i],
            device_id=to(shift), device_id_type=MESH,
        )

    v1_up = [v_up(blocks[j], 1, j) for j in order]
    v1_over = [v_over(blocks[j], blocks[3 + j], 7 + j, j, -3) for j in order]
    v2_up = [v_up(blocks[j], 3, j) for j in order[:3]]
    v2_over = [v_over(blocks[j], blocks[j - 1], 10 + j, j, -2) for j in order[:3]]

    @pl.when(v_far & odd)
    def _():
        for copy in v1_up:
            copy.start()

    @pl.when(v_far & even)
    def _():
        for copy in v2_up:
            copy.start()

    @pl.when(next1 & jnp.logical_not(v_far & odd))
    def _():
        start(v1)

    @pl.when(next2 & even & jnp.logical_not(v_far))
    def _():
        start(v2)

    for load in (load_q, load_k, load_g, load_v):
        load.start()

    @pl.when(jnp.logical_not(prev1))
    def _():
        kwin[one] = jnp.zeros((TOK, HD), BF16)
        vwin[one] = jnp.zeros((TOK, HD), BF16)

    @pl.when(jnp.logical_not(prev2))
    def _():
        kwin[two] = jnp.zeros((3 * BLK, HD), BF16)
        vwin[two] = jnp.zeros((3 * BLK, HD), BF16)

    def cut(i):
        return slice(i * BLK, (i + 1) * BLK)

    def cols(b):
        return slice(b * COLS, (b + 1) * COLS)

    def split(src, stacked, turned):
        for b in range(NB):
            for h in range(HEADS):
                x = src[cut(b), cut(h)]
                at = slice(b * COLS + h * BLK, b * COLS + (h + 1) * BLK)
                stacked[at, :] = x
                turned[:, at] = x.T

    def turn(src, dst, rows):
        dst[:, rows] = src[rows, :].T

    causal = lax.broadcasted_iota(jnp.int32, (BLK, COLS), 0) <= lax.rem(
        lax.broadcasted_iota(jnp.int32, (BLK, COLS), 1), BLK
    )

    def score(w, b):
        x = dot(kwin[cut(w), :], q_t[:, cols(b)])
        if w == b + 7:
            x = jnp.where(causal, x, -1e30)
        m = jnp.max(x, axis=0, keepdims=True)
        e = jnp.exp2((x - m) * SCALE2)
        top[w : w + 1, cols(b)] = m
        total[w : w + 1, cols(b)] = jnp.sum(e, axis=0, keepdims=True)
        e_all[cut(w), cols(b)] = e

    def reach(w):
        return [b for b in range(NB) if b <= w <= b + 7]

    load_q.wait()
    split(q_in, q_s, q_t)
    load_k.wait()
    for w in range(7, 11):
        for b in reach(w):
            score(w, b)
    turn(kwin, k_t, slice(OWN, OWN + TOK))
    load_g.wait()
    split(g_in, g_s, g_t)
    load_v.wait()
    turn(vwin, v_t, slice(OWN, OWN + TOK))
    for w in range(7, 11):
        for b in reach(w):
            dp_own[cut(w - 7), cols(b)] = dot(vwin[cut(w), :], g_t[:, cols(b)])

    def score_one(j):
        arrived_one(k1, k2_on, j)
        for b in range(NB):
            score(3 + j, b)

    def score_two(j):
        arrived_two(k2, j)
        for b in reach(j - 1):
            score(j - 1, b)

    score_one(1)
    score_one(2)
    score_two(1)
    score_one(3)
    score_two(2)
    score_two(3)
    score_one(0)
    turn(kwin, k_t, slice(0, OWN))

    for b in range(NB):
        mine = docs[s * NB + b]
        ws = range(b, b + 8)
        alike = []
        for w in ws:
            at = s * NB + (w - 7)
            alike.append((docs[jnp.maximum(at, 0)] == mine) & (at >= 0))
        tops = [top[w : w + 1, cols(b)] for w in ws]
        high = tops[-1]
        for t, ok in zip(tops[:-1], alike[:-1]):
            high = jnp.maximum(high, jnp.where(ok, t, -1e30))
        alphas = [
            jnp.where(ok, jnp.exp2((t - high) * SCALE2), 0.0) for t, ok in zip(tops, alike)
        ]
        whole = sum(a * total[w : w + 1, cols(b)] for a, w in zip(alphas, ws))
        inverse = 1.0 / whole
        for a, w in zip(alphas, ws):
            alpha[w : w + 1, cols(b)] = a * inverse

    def prob(w, b):
        p_all[cut(w), cols(b)] = (e_all[cut(w), cols(b)] * alpha[w : w + 1, cols(b)]).astype(BF16)

    def gather(pairs, other, w):
        bs = reach(w)
        at = slice(bs[0] * COLS, (bs[-1] + 1) * COLS)
        return dot(pairs[cut(w), at], other[at, :])

    def back(src, dst, i, shift):
        return pltpu.make_async_remote_copy(
            src, dst, back_send.at[i], back_recv.at[i], device_id=to(shift), device_id_type=MESH
        )

    pv1 = back(pv.at[one], rv1, 0, -1)
    pv2 = back(pv.at[two], rv2, 1, -2)
    pk1 = back(pk.at[one], rk1, 2, -1)
    pk2 = back(pk.at[two], rk2, 3, -2)

    def hop(src, dst, i):
        return pltpu.make_async_remote_copy(
            src, dst, back_send.at[i], hop_recv.at[i],
            device_id=to(-4), device_id_type=MESH,
        )

    def over(src, dst, i, shift):
        return pltpu.make_async_remote_copy(
            src, dst, hop_send.at[i], back_recv.at[i], device_id=to(shift), device_id_type=MESH
        )

    pv1_hop = hop(pv.at[one], pv_hop.at[one], 0)
    pv2_hop = hop(pv.at[two], pv_hop.at[two], 1)
    pk1_hop = hop(pk.at[one], pk_hop.at[one], 2)
    pk2_hop = hop(pk.at[two], pk_hop.at[two], 3)
    pv1_over = over(pv_hop.at[one], rv1, 0, 3)
    pv2_over = over(pv_hop.at[two], rv2, 1, 2)
    pk1_over = over(pk_hop.at[one], rk1, 2, 3)
    pk2_over = over(pk_hop.at[two], rk2, 3, 2)

    for w in range(3):
        for b in reach(w):
            prob(w, b)
    for w in range(3):
        pv[cut(w), :] = gather(p_all, g_s, w).astype(BF16)

    @pl.when(first)
    def _():
        pl.semaphore_wait(ready, 1)
        pv2_hop.start()

    @pl.when(prev2 & jnp.logical_not(first))
    def _():
        pv2.start()

    for w in range(3, 7):
        for b in range(NB):
            prob(w, b)
    for w in range(3, 7):
        pv[cut(w), :] = gather(p_all, g_s, w).astype(BF16)

    @pl.when(first & even)
    def _():
        pv1_hop.start()

    @pl.when(prev1 & jnp.logical_not(first & even))
    def _():
        pv1.start()

    for j in order:
        arrived_one(v1, v2_on, j)
    for w in range(7, 11):
        for b in reach(w):
            prob(w, b)
    for b in range(NB):
        keys = slice(OWN, OWN + (b + 1) * BLK)
        out_own[:, cols(b)] = dot(v_t[:, keys], p_all[keys, cols(b)])
    turn(vwin, v_t, slice(ONE, ONE + TOK))

    for j in order[:3]:
        arrived_two(v2, j)

    turn(vwin, v_t, slice(0, 3 * BLK))

    def home(dst, b, x):
        for h in range(HEADS):
            dst[cut(b), cut(h)] = x[:, cut(h)].T

    for b in range(NB):
        keys = slice(b * BLK, OWN)
        out = (dot(v_t[:, keys], p_all[keys, cols(b)]) + out_own[:, cols(b)]).astype(BF16)
        delta[0:1, cols(b)] = jnp.sum(
            g_t[:, cols(b)].astype(F32) * out.astype(F32), axis=0, keepdims=True
        )
        home(att_out, b, out)

    def dscore(w, b):
        if w < 7:
            dp = dot(vwin[cut(w), :], g_t[:, cols(b)])
        else:
            dp = dp_own[cut(w - 7), cols(b)]
        d_all[cut(w), cols(b)] = (
            p_all[cut(w), cols(b)].astype(F32) * (dp - delta[0:1, cols(b)])
        ).astype(BF16)

    for w in range(7):
        for b in reach(w):
            dscore(w, b)
    for w in range(3, 7):
        pk[cut(w), :] = (gather(d_all, q_s, w) * SCALE).astype(BF16)

    @pl.when(first & even)
    def _():
        pk1_hop.start()

    @pl.when(prev1 & jnp.logical_not(first & even))
    def _():
        pk1.start()

    for w in range(3):
        pk[cut(w), :] = (gather(d_all, q_s, w) * SCALE).astype(BF16)

    @pl.when(first)
    def _():
        pk2_hop.start()

    @pl.when(prev2 & jnp.logical_not(first))
    def _():
        pk2.start()

    for w in range(7, 11):
        for b in reach(w):
            dscore(w, b)
    for b in range(NB):
        keys = slice(b * BLK, (b + 8) * BLK)
        home(qg_out, b, (dot(k_t[:, keys], d_all[keys, cols(b)]) * SCALE).astype(BF16))
    for w in range(7, 11):
        dk_own[cut(w - 7), :] = gather(d_all, q_s, w) * SCALE
        dv_own[cut(w - 7), :] = gather(p_all, g_s, w)

    @pl.when(v_passes & odd)
    def _():
        for arrives, leaves in zip(v1_up, v1_over):
            arrives.wait_recv()
            leaves.start()

    @pl.when(v_passes & even)
    def _():
        for arrives, leaves in zip(v2_up, v2_over):
            arrives.wait_recv()
            leaves.start()

    @pl.when(passes & even)
    def _():
        pv1_hop.wait_recv()
        pv1_over.start()

    @pl.when(passes)
    def _():
        pv2_hop.wait_recv()
        pv2_over.start()

    @pl.when(passes & even)
    def _():
        pk1_hop.wait_recv()
        pk1_over.start()

    @pl.when(passes)
    def _():
        pk2_hop.wait_recv()
        pk2_over.start()

    @pl.when(next1)
    def _():
        pv1.wait_recv()
        dv_own[...] += rv1[...].astype(F32)

    @pl.when(next2)
    def _():
        pv2.wait_recv()
        dv_own[tail] += rv2[...].astype(F32)

    vg_out[...] = dv_own[...].astype(BF16)

    @pl.when(next1)
    def _():
        pk1.wait_recv()
        dk_own[...] += rk1[...].astype(F32)

    @pl.when(next2)
    def _():
        pk2.wait_recv()
        dk_own[tail] += rk2[...].astype(F32)

    kg_out[...] = dk_own[...].astype(BF16)

    @pl.when(next1)
    def _():
        left(k1)
        left(v1)

    @pl.when(next2 & even)
    def _():
        left(k2)
        left(v2)

    @pl.when(prev1 & next1 & even)
    def _():
        left(k2_on)
        left(v2_on)

    @pl.when(prev1)
    def _():
        pv1.wait_send()
        pk1.wait_send()

    @pl.when(prev2)
    def _():
        pv2.wait_send()
        pk2.wait_send()

    @pl.when(v_passes & odd)
    def _():
        for copy in v1_over:
            copy.wait_send()

    @pl.when(v_passes & even)
    def _():
        for copy in v2_over:
            copy.wait_send()

    @pl.when(passes & even)
    def _():
        pv1_over.wait_send()
        pk1_over.wait_send()

    @pl.when(passes)
    def _():
        pv2_over.wait_send()
        pk2_over.wait_send()


def place(*refs):
    sems = refs[-1]
    half = (len(refs) - 1) // 2
    stores = [
        pltpu.make_async_copy(refs[i], refs[half + i], sems.at[i]) for i in range(half)
    ]
    for store in stores:
        store.start()
    for store in stores:
        store.wait()


def body(n, queries, key_vecs, value_vecs, out_grad, doc_ids):
    def buf(rows, columns, kind=BF16):
        return pltpu.VMEM((rows, columns), kind)

    wide = NB * COLS
    anywhere = pl.BlockSpec(memory_space=pl.ANY)
    in_vmem = pl.BlockSpec(memory_space=pltpu.VMEM)
    sizes = [(TOK, HEADS * HD), (TOK, HEADS * HD), (TOK, HD), (TOK, HD)]
    results = pl.pallas_call(
        functools.partial(kernel, n),
        name="attention",
        out_shape=[pltpu.VMEM(size, BF16) for size in sizes],
        in_specs=[pl.BlockSpec(memory_space=pltpu.SMEM)] + [anywhere] * 4,
        out_specs=[in_vmem] * 4,
        scratch_shapes=[
            buf(TOK, HEADS * HD), buf(TOK, HEADS * HD),
            buf(WIN * BLK, HD), buf(WIN * BLK, HD), buf(HD, WIN * BLK), buf(HD, WIN * BLK),
            buf(HD, wide), buf(HD, wide), buf(wide, HD), buf(wide, HD),
            buf(WIN * BLK, wide, F32), buf(WIN * BLK, wide), buf(WIN * BLK, wide),
            buf(TOK, wide, F32), buf(HD, wide, F32),
            buf(16, wide, F32), buf(16, wide, F32), buf(16, wide, F32), buf(8, wide, F32),
            buf(TOK, HD, F32), buf(TOK, HD, F32),
            buf(7 * BLK, HD), buf(7 * BLK, HD),
            buf(TOK, HD), buf(3 * BLK, HD), buf(TOK, HD), buf(3 * BLK, HD),
            pltpu.SemaphoreType.DMA((4,)), pltpu.SemaphoreType.DMA((6,)), pltpu.SemaphoreType.DMA((14,)),
            pltpu.SemaphoreType.DMA((4,)), pltpu.SemaphoreType.DMA((4,)),
            buf(TOK, HD), buf(7 * BLK, HD), buf(7 * BLK, HD),
            pltpu.SemaphoreType.DMA((4,)), pltpu.SemaphoreType.DMA((4,)),
            pltpu.SemaphoreType.DMA((4,)), pltpu.SemaphoreType.DMA((4,)),
            pltpu.SemaphoreType.REGULAR,
        ],
        compiler_params=pltpu.CompilerParams(
            collective_id=0, has_side_effects=True, vmem_limit_bytes=56 * 1024 * 1024
        ),
        cost_estimate=pl.CostEstimate(
            flops=2 * 6 * 32 * HEADS * BLK**3, bytes_accessed=5 * TOK * TOK, transcendentals=2**21
        ),
    )(doc_ids, queries, key_vecs, value_vecs, out_grad)
    results = [pltpu.with_memory_space_constraint(r, pltpu.VMEM) for r in results]
    return pl.pallas_call(
        place,
        name="place",
        out_shape=[jax.ShapeDtypeStruct(size, BF16) for size in sizes],
        in_specs=[in_vmem] * 4,
        out_specs=[anywhere] * 4,
        scratch_shapes=[pltpu.SemaphoreType.DMA((4,))],
    )(*results)


def solution(mesh):
    placed = P("ctx", "tp")
    return jax.shard_map(
        functools.partial(body, mesh.shape["ctx"]),
        mesh=mesh,
        in_specs=(placed,) * 4 + (P(),),
        out_specs=(placed,) * 4,
        check_vma=False,
    )
```

```python
import functools
import math

import jax
import jax.numpy as jnp
from jax import lax
from jax.experimental import pallas as pl
from jax.experimental.pallas import tpu as pltpu
from jax.sharding import PartitionSpec as P

HD = 128
BLK = 128
HEADS = 4
NB = 4
TOK = NB * BLK
WIN = 11
COLS = HEADS * BLK
COLUMN = 24
OWN = 7 * BLK
ONE = 3 * BLK
SCALE = HD**-0.5
SCALE2 = SCALE * math.log2(math.e)
MESH = pl.DeviceIdType.MESH
F32 = jnp.float32
BF16 = jnp.bfloat16


def dot(a, b):
    return jnp.dot(a, b, preferred_element_type=F32)


def kernel(
    n,
    docs, q_hbm, k_hbm, v_hbm, g_hbm,
    att_out, qg_out, kg_out, vg_out,
    q_in, g_in,
    kwin, vwin, k_t, v_t, q_t, g_t, q_s, g_s,
    e_all, p_all, d_all, dp_own, out_own, top, total, alpha, delta,
    dk_own, dv_own, pk, pv, rk1, rk2, rv1, rv2,
    load_sem, send_sem, recv_sem, back_send, back_recv,
    v_hop, pv_hop, pk_hop, v_hop_send, v_hop_recv, hop_send, hop_recv, ready,
):
    s = lax.axis_index("ctx")
    even = lax.rem(s, 2) == 0
    odd = lax.rem(s, 2) == 1
    prev1, prev2, next1, next2 = s >= 1, s >= 2, s + 1 < n, s + 2 < n
    place_in = lax.rem(s, COLUMN)
    high = lax.rem(lax.axis_index("tp"), 2) == 1
    first = high & (place_in < 2) & (s >= COLUMN)
    v_passes = high & (place_in >= 2) & (place_in < 4) & (s >= COLUMN)
    passes = high & (place_in >= COLUMN - 4) & (place_in < COLUMN - 2) & (s + 4 < n)
    v_far = high & (place_in >= COLUMN - 2) & (s + 4 < n)

    def to(shift):
        return {"ctx": lax.rem(s + shift + n, n)}

    barrier = pltpu.get_barrier_semaphore()

    @pl.when(prev1)
    def _():
        pl.semaphore_signal(barrier, inc=1, device_id=to(-1), device_id_type=MESH)

    @pl.when(prev2 & even)
    def _():
        pl.semaphore_signal(barrier, inc=1, device_id=to(-2), device_id_type=MESH)

    @pl.when(first | v_passes)
    def _():
        pl.semaphore_signal(barrier, inc=1, device_id=to(-4), device_id_type=MESH)

    own = pl.ds(OWN, TOK)
    load_q = pltpu.make_async_copy(q_hbm, q_in, load_sem.at[0])
    load_k = pltpu.make_async_copy(k_hbm, kwin.at[own], load_sem.at[1])
    load_v = pltpu.make_async_copy(v_hbm, vwin.at[own], load_sem.at[2])
    load_g = pltpu.make_async_copy(g_hbm, g_in, load_sem.at[3])

    targets = sum(
        x.astype(jnp.int32) for x in (next1, next2 & even, passes, v_far)
    )

    @pl.when(targets > 0)
    def _():
        pl.semaphore_wait(barrier, targets)

    @pl.when(passes)
    def _():
        pl.semaphore_signal(ready, inc=1, device_id=to(4), device_id_type=MESH)

    def send(src, dst, i, arrival, shift):
        return pltpu.make_async_remote_copy(
            src, dst, send_sem.at[i], recv_sem.at[arrival],
            device_id=to(shift), device_id_type=MESH,
        )

    blocks = [pl.ds(j * BLK, BLK) for j in range(7)]
    tail = pl.ds(BLK, 3 * BLK)
    one, two = pl.ds(ONE, TOK), pl.ds(0, 3 * BLK)
    order = (1, 2, 3, 0)

    def stream(hbm, win, i):
        to_one = {j: send(hbm.at[blocks[j]], win.at[blocks[3 + j]], i, 7 * i + j, 1) for j in order}
        to_two = {
            j: send(hbm.at[blocks[j]], win.at[blocks[j - 1]], 2 + i, 7 * i + 3 + j, 2)
            for j in order[:3]
        }
        onward = {
            j: send(win.at[blocks[3 + j]], win.at[blocks[j - 1]], 4 + i, 7 * i + 3 + j, 1)
            for j in order[:3]
        }
        return to_one, to_two, onward

    k1, k2, k2_on = stream(k_hbm, kwin, 0)
    v1, v2, v2_on = stream(v_hbm, vwin, 1)

    def start(copies):
        for copy in copies.values():
            copy.start()

    def left(copies):
        for copy in copies.values():
            copy.wait_send()

    def arrived_one(copies, onward, j):
        @pl.when(prev1)
        def _():
            copies[j].wait_recv()

        if j > 0:

            @pl.when(prev1 & next1 & even)
            def _():
                onward[j].start()

    def arrived_two(copies, j):
        @pl.when(prev2)
        def _():
            copies[j].wait_recv()

    @pl.when(next1)
    def _():
        start(k1)

    @pl.when(next2 & even)
    def _():
        start(k2)

    def v_up(src, i, j):
        return pltpu.make_async_remote_copy(
            v_hbm.at[src], v_hop.at[src], send_sem.at[i], v_hop_recv.at[j],
            device_id=to(4), device_id_type=MESH,
        )

    def v_over(src, dst, i, j, shift):
        return pltpu.make_async_remote_copy(
            v_hop.at[src], vwin.at[dst], v_hop_send.at[j], recv_sem.at[i],
            device_id=to(shift), device_id_type=MESH,
        )

    v1_up = [v_up(blocks[j], 1, j) for j in order]
    v1_over = [v_over(blocks[j], blocks[3 + j], 7 + j, j, -3) for j in order]
    v2_up = [v_up(blocks[j], 3, j) for j in order[:3]]
    v2_over = [v_over(blocks[j], blocks[j - 1], 10 + j, j, -2) for j in order[:3]]

    @pl.when(v_far & odd)
    def _():
        for copy in v1_up:
            copy.start()

    @pl.when(v_far & even)
    def _():
        for copy in v2_up:
            copy.start()

    @pl.when(next1 & jnp.logical_not(v_far & odd))
    def _():
        start(v1)

    @pl.when(next2 & even & jnp.logical_not(v_far))
    def _():
        start(v2)

    for load in (load_q, load_k, load_g, load_v):
        load.start()

    @pl.when(jnp.logical_not(prev1))
    def _():
        kwin[one] = jnp.zeros((TOK, HD), BF16)
        vwin[one] = jnp.zeros((TOK, HD), BF16)

    @pl.when(jnp.logical_not(prev2))
    def _():
        kwin[two] = jnp.zeros((3 * BLK, HD), BF16)
        vwin[two] = jnp.zeros((3 * BLK, HD), BF16)

    def cut(i):
        return slice(i * BLK, (i + 1) * BLK)

    def cols(b):
        return slice(b * COLS, (b + 1) * COLS)

    def split(src, stacked, turned):
        for b in range(NB):
            for h in range(HEADS):
                x = src[cut(b), cut(h)]
                at = slice(b * COLS + h * BLK, b * COLS + (h + 1) * BLK)
                stacked[at, :] = x
                turned[:, at] = x.T

    def turn(src, dst, rows):
        dst[:, rows] = src[rows, :].T

    causal = lax.broadcasted_iota(jnp.int32, (BLK, COLS), 0) <= lax.rem(
        lax.broadcasted_iota(jnp.int32, (BLK, COLS), 1), BLK
    )

    def score(w, b):
        x = dot(kwin[cut(w), :], q_t[:, cols(b)])
        if w == b + 7:
            x = jnp.where(causal, x, -1e30)
        m = jnp.max(x, axis=0, keepdims=True)
        e = jnp.exp2((x - m) * SCALE2)
        top[w : w + 1, cols(b)] = m
        total[w : w + 1, cols(b)] = jnp.sum(e, axis=0, keepdims=True)
        e_all[cut(w), cols(b)] = e

    def reach(w):
        return [b for b in range(NB) if b <= w <= b + 7]

    load_q.wait()
    split(q_in, q_s, q_t)
    load_k.wait()
    for w in range(7, 11):
        for b in reach(w):
            score(w, b)
    turn(kwin, k_t, slice(OWN, OWN + TOK))
    load_g.wait()
    split(g_in, g_s, g_t)
    load_v.wait()
    turn(vwin, v_t, slice(OWN, OWN + TOK))
    for w in range(7, 11):
        for b in reach(w):
            dp_own[cut(w - 7), cols(b)] = dot(vwin[cut(w), :], g_t[:, cols(b)])

    def score_one(j):
        arrived_one(k1, k2_on, j)
        for b in range(NB):
            score(3 + j, b)

    def score_two(j):
        arrived_two(k2, j)
        for b in reach(j - 1):
            score(j - 1, b)

    score_one(1)
    score_one(2)
    score_two(1)
    score_one(3)
    score_two(2)
    score_two(3)
    score_one(0)
    turn(kwin, k_t, slice(0, OWN))

    for b in range(NB):
        mine = docs[s * NB + b]
        ws = range(b, b + 8)
        alike = []
        for w in ws:
            at = s * NB + (w - 7)
            alike.append((docs[jnp.maximum(at, 0)] == mine) & (at >= 0))
        tops = [top[w : w + 1, cols(b)] for w in ws]
        high = tops[-1]
        for t, ok in zip(tops[:-1], alike[:-1]):
            high = jnp.maximum(high, jnp.where(ok, t, -1e30))
        alphas = [
            jnp.where(ok, jnp.exp2((t - high) * SCALE2), 0.0) for t, ok in zip(tops, alike)
        ]
        whole = sum(a * total[w : w + 1, cols(b)] for a, w in zip(alphas, ws))
        inverse = 1.0 / whole
        for a, w in zip(alphas, ws):
            alpha[w : w + 1, cols(b)] = a * inverse

    def prob(w, b):
        p_all[cut(w), cols(b)] = (e_all[cut(w), cols(b)] * alpha[w : w + 1, cols(b)]).astype(BF16)

    def gather(pairs, other, w):
        bs = reach(w)
        at = slice(bs[0] * COLS, (bs[-1] + 1) * COLS)
        return dot(pairs[cut(w), at], other[at, :])

    def back(src, dst, i, shift):
        return pltpu.make_async_remote_copy(
            src, dst, back_send.at[i], back_recv.at[i], device_id=to(shift), device_id_type=MESH
        )

    pv1 = back(pv.at[one], rv1, 0, -1)
    pv2 = back(pv.at[two], rv2, 1, -2)
    pk1 = back(pk.at[one], rk1, 2, -1)
    pk2 = back(pk.at[two], rk2, 3, -2)

    def leave(part, one_dst, hop_dst, i, w):
        direct = back(part.at[blocks[w]], one_dst.at[blocks[w - 3]], i, -1)
        by_hop = hop(part.at[blocks[w]], hop_dst.at[blocks[w]], i)

        @pl.when(first & even)
        def _():
            by_hop.start()

        @pl.when(prev1 & jnp.logical_not(first & even))
        def _():
            direct.start()

    def hop(src, dst, i):
        return pltpu.make_async_remote_copy(
            src, dst, back_send.at[i], hop_recv.at[i],
            device_id=to(-4), device_id_type=MESH,
        )

    def over(src, dst, i, shift):
        return pltpu.make_async_remote_copy(
            src, dst, hop_send.at[i], back_recv.at[i], device_id=to(shift), device_id_type=MESH
        )

    pv1_hop = hop(pv.at[one], pv_hop.at[one], 0)
    pv2_hop = hop(pv.at[two], pv_hop.at[two], 1)
    pk1_hop = hop(pk.at[one], pk_hop.at[one], 2)
    pk2_hop = hop(pk.at[two], pk_hop.at[two], 3)
    pv1_over = over(pv_hop.at[one], rv1, 0, 3)
    pv2_over = over(pv_hop.at[two], rv2, 1, 2)
    pk1_over = over(pk_hop.at[one], rk1, 2, 3)
    pk2_over = over(pk_hop.at[two], rk2, 3, 2)

    for w in range(3):
        for b in reach(w):
            prob(w, b)
    for w in range(3):
        pv[cut(w), :] = gather(p_all, g_s, w).astype(BF16)

    @pl.when(first)
    def _():
        pl.semaphore_wait(ready, 1)
        pv2_hop.start()

    @pl.when(prev2 & jnp.logical_not(first))
    def _():
        pv2.start()

    for w in range(3, 7):
        for b in range(NB):
            prob(w, b)
        pv[cut(w), :] = gather(p_all, g_s, w).astype(BF16)
        leave(pv, rv1, pv_hop, 0, w)
        if w == 4:
            arrived_one(v1, v2_on, 1)
            arrived_one(v1, v2_on, 2)
    arrived_one(v1, v2_on, 3)
    arrived_one(v1, v2_on, 0)
    for w in range(7, 11):
        for b in reach(w):
            prob(w, b)
    for b in range(NB):
        keys = slice(OWN, OWN + (b + 1) * BLK)
        out_own[:, cols(b)] = dot(v_t[:, keys], p_all[keys, cols(b)])
    turn(vwin, v_t, slice(ONE, ONE + TOK))

    for j in order[:3]:
        arrived_two(v2, j)

    turn(vwin, v_t, slice(0, 3 * BLK))

    def home(dst, b, x):
        for h in range(HEADS):
            dst[cut(b), cut(h)] = x[:, cut(h)].T

    for b in range(NB):
        keys = slice(b * BLK, OWN)
        out = (dot(v_t[:, keys], p_all[keys, cols(b)]) + out_own[:, cols(b)]).astype(BF16)
        delta[0:1, cols(b)] = jnp.sum(
            g_t[:, cols(b)].astype(F32) * out.astype(F32), axis=0, keepdims=True
        )
        home(att_out, b, out)

    def dscore(w, b):
        if w < 7:
            dp = dot(vwin[cut(w), :], g_t[:, cols(b)])
        else:
            dp = dp_own[cut(w - 7), cols(b)]
        d_all[cut(w), cols(b)] = (
            p_all[cut(w), cols(b)].astype(F32) * (dp - delta[0:1, cols(b)])
        ).astype(BF16)

    for w in range(3):
        for b in reach(w):
            dscore(w, b)

    for w in range(3):
        pk[cut(w), :] = (gather(d_all, q_s, w) * SCALE).astype(BF16)

    @pl.when(first)
    def _():
        pk2_hop.start()

    @pl.when(prev2 & jnp.logical_not(first))
    def _():
        pk2.start()

    for w in range(3, 7):
        for b in range(NB):
            dscore(w, b)
        pk[cut(w), :] = (gather(d_all, q_s, w) * SCALE).astype(BF16)
        leave(pk, rk1, pk_hop, 2, w)

    for w in range(7, 11):
        for b in reach(w):
            dscore(w, b)
    for b in range(NB):
        keys = slice(b * BLK, (b + 8) * BLK)
        home(qg_out, b, (dot(k_t[:, keys], d_all[keys, cols(b)]) * SCALE).astype(BF16))
    for w in range(7, 11):
        dk_own[cut(w - 7), :] = gather(d_all, q_s, w) * SCALE
        dv_own[cut(w - 7), :] = gather(p_all, g_s, w)

    @pl.when(v_passes & odd)
    def _():
        for arrives, leaves in zip(v1_up, v1_over):
            arrives.wait_recv()
            leaves.start()

    @pl.when(v_passes & even)
    def _():
        for arrives, leaves in zip(v2_up, v2_over):
            arrives.wait_recv()
            leaves.start()

    @pl.when(passes & even)
    def _():
        pv1_hop.wait_recv()
        pv1_over.start()

    @pl.when(passes)
    def _():
        pv2_hop.wait_recv()
        pv2_over.start()

    @pl.when(passes & even)
    def _():
        pk1_hop.wait_recv()
        pk1_over.start()

    @pl.when(passes)
    def _():
        pk2_hop.wait_recv()
        pk2_over.start()

    @pl.when(next1)
    def _():
        pv1.wait_recv()
        dv_own[...] += rv1[...].astype(F32)

    @pl.when(next2)
    def _():
        pv2.wait_recv()
        dv_own[tail] += rv2[...].astype(F32)

    vg_out[...] = dv_own[...].astype(BF16)

    @pl.when(next1)
    def _():
        pk1.wait_recv()
        dk_own[...] += rk1[...].astype(F32)

    @pl.when(next2)
    def _():
        pk2.wait_recv()
        dk_own[tail] += rk2[...].astype(F32)

    kg_out[...] = dk_own[...].astype(BF16)

    @pl.when(next1)
    def _():
        left(k1)
        left(v1)

    @pl.when(next2 & even)
    def _():
        left(k2)
        left(v2)

    @pl.when(prev1 & next1 & even)
    def _():
        left(k2_on)
        left(v2_on)

    @pl.when(prev1)
    def _():
        pv1.wait_send()
        pk1.wait_send()

    @pl.when(prev2)
    def _():
        pv2.wait_send()
        pk2.wait_send()

    @pl.when(v_passes & odd)
    def _():
        for copy in v1_over:
            copy.wait_send()

    @pl.when(v_passes & even)
    def _():
        for copy in v2_over:
            copy.wait_send()

    @pl.when(passes & even)
    def _():
        pv1_over.wait_send()
        pk1_over.wait_send()

    @pl.when(passes)
    def _():
        pv2_over.wait_send()
        pk2_over.wait_send()


def place(*refs):
    sems = refs[-1]
    half = (len(refs) - 1) // 2
    stores = [
        pltpu.make_async_copy(refs[i], refs[half + i], sems.at[i]) for i in range(half)
    ]
    for store in stores:
        store.start()
    for store in stores:
        store.wait()


def body(n, queries, key_vecs, value_vecs, out_grad, doc_ids):
    def buf(rows, columns, kind=BF16):
        return pltpu.VMEM((rows, columns), kind)

    wide = NB * COLS
    anywhere = pl.BlockSpec(memory_space=pl.ANY)
    in_vmem = pl.BlockSpec(memory_space=pltpu.VMEM)
    sizes = [(TOK, HEADS * HD), (TOK, HEADS * HD), (TOK, HD), (TOK, HD)]
    results = pl.pallas_call(
        functools.partial(kernel, n),
        name="attention",
        out_shape=[pltpu.VMEM(size, BF16) for size in sizes],
        in_specs=[pl.BlockSpec(memory_space=pltpu.SMEM)] + [anywhere] * 4,
        out_specs=[in_vmem] * 4,
        scratch_shapes=[
            buf(TOK, HEADS * HD), buf(TOK, HEADS * HD),
            buf(WIN * BLK, HD), buf(WIN * BLK, HD), buf(HD, WIN * BLK), buf(HD, WIN * BLK),
            buf(HD, wide), buf(HD, wide), buf(wide, HD), buf(wide, HD),
            buf(WIN * BLK, wide, F32), buf(WIN * BLK, wide), buf(WIN * BLK, wide),
            buf(TOK, wide, F32), buf(HD, wide, F32),
            buf(16, wide, F32), buf(16, wide, F32), buf(16, wide, F32), buf(8, wide, F32),
            buf(TOK, HD, F32), buf(TOK, HD, F32),
            buf(7 * BLK, HD), buf(7 * BLK, HD),
            buf(TOK, HD), buf(3 * BLK, HD), buf(TOK, HD), buf(3 * BLK, HD),
            pltpu.SemaphoreType.DMA((4,)), pltpu.SemaphoreType.DMA((6,)), pltpu.SemaphoreType.DMA((14,)),
            pltpu.SemaphoreType.DMA((4,)), pltpu.SemaphoreType.DMA((4,)),
            buf(TOK, HD), buf(7 * BLK, HD), buf(7 * BLK, HD),
            pltpu.SemaphoreType.DMA((4,)), pltpu.SemaphoreType.DMA((4,)),
            pltpu.SemaphoreType.DMA((4,)), pltpu.SemaphoreType.DMA((4,)),
            pltpu.SemaphoreType.REGULAR,
        ],
        compiler_params=pltpu.CompilerParams(
            collective_id=0, has_side_effects=True, vmem_limit_bytes=56 * 1024 * 1024
        ),
        cost_estimate=pl.CostEstimate(
            flops=2 * 6 * 32 * HEADS * BLK**3, bytes_accessed=5 * TOK * TOK, transcendentals=2**21
        ),
    )(doc_ids, queries, key_vecs, value_vecs, out_grad)
    results = [pltpu.with_memory_space_constraint(r, pltpu.VMEM) for r in results]
    return pl.pallas_call(
        place,
        name="place",
        out_shape=[jax.ShapeDtypeStruct(size, BF16) for size in sizes],
        in_specs=[in_vmem] * 4,
        out_specs=[anywhere] * 4,
        scratch_shapes=[pltpu.SemaphoreType.DMA((4,))],
    )(*results)


def solution(mesh):
    placed = P("ctx", "tp")
    return jax.shard_map(
        functools.partial(body, mesh.shape["ctx"]),
        mesh=mesh,
        in_specs=(placed,) * 4 + (P(),),
        out_specs=(placed,) * 4,
        check_vma=False,
    )
```
